256 devices in a mesh: ctx: 16 (over z_lo, x, core), ch: 16 (over z_hi, y).
Axes of the slice: x: 4, y: 4, z: 8 (z_hi: 4, z_lo: 2; z = z_hi * 2 + z_lo), core: 2. Of those that a mesh axis runs over, the one named last changes fastest.
Arguments:
- seq_input: bfloat16 [32768, 2048], P('ctx', 'ch'), may hold values from -6 to 6
- out_grad: bfloat16 [32768, 2048], P('ctx', 'ch'), may hold values from -6 to 6
- filters: bfloat16 [32768, 128], P('ctx', 'ch'), may hold values from -1.1 to 1.1
Outputs:
- conv_out: bfloat16 [32768, 2048], P('ctx', 'ch')
- input_grad: bfloat16 [32768, 2048], P('ctx', 'ch')
- filter_grad: float32 [32768, 128], P('ctx')
The draws below stay inside these ranges and needn't reach their ends.
All inputs are finite; a program needn't handle non-finite values.
Results may differ from the reference program's by a relative error of at most 0.02.
Values may be sent and summed in bfloat16 or wider, within the bound.
No kernel may reach another device: no remote copies, remote signals or barrier semaphores. Data moves between devices by JAX's collectives and lax.ppermute only.
A program may use at most 128 MiB of HBM per device.

```python
import math
import jax
import jax.numpy as jnp
from jax import lax

P_SIZE = 256
G = 128
C = 2048
TOKENS = 32768
Q = 256
N_CH = 16


def draw_filters(key, part):
    key = jax.random.fold_in(key, 11)
    key_rate, key_rough = jax.random.split(key)
    positions = jnp.arange(TOKENS, dtype=jnp.float32)[:, None]
    lengths = jnp.exp(jax.random.uniform(key_rate, (G,), jnp.float32, math.log(30.0), math.log(TOKENS * 4.0)))
    rough_part = jax.random.truncated_normal(key_rough, -4.0, 4.0, (TOKENS, G), jnp.float32)
    decay_rate = 1.0 / lengths
    amplitude = jnp.sqrt(-jnp.expm1(-2.0 * decay_rate) / -jnp.expm1(-2.0 * decay_rate * TOKENS))
    return (rough_part * amplitude * jnp.exp(-positions * decay_rate)).astype(jnp.bfloat16)


def level_of(own_key, extent, cuts, smallest, top_value):
    loudness, own = 1.0, jax.random.fold_in(own_key, 6)
    for axis_at, parts in cuts:
        heights = jnp.exp(jax.random.uniform(jax.random.fold_in(own, axis_at), (parts,), jnp.float32, smallest / len(cuts), top_value / len(cuts)))
        loudness = loudness * jnp.repeat(heights, extent[axis_at] // parts).reshape([-1 if axis == axis_at else 1 for axis in range(len(extent))])
    return loudness


def centred(key, shape, spread, bound, pieces=(), held_as=jnp.bfloat16):
    factor_of = level_of(key, shape, pieces, -0.22, 0.18) if pieces else 1.0
    values = jax.random.normal(key, shape, jnp.float32) * spread * factor_of
    return jnp.minimum(jnp.maximum(values, -bound), bound).astype(held_as)


def setup_inputs(seed: int = 0) -> dict:
    splits = jax.random.split(jax.random.key(seed), 4)
    return {
        "seq_input": centred(splits[0], (TOKENS, C), 1.0, 6.0, ((0, 16), (1, 16))),
        "out_grad": centred(splits[1], (TOKENS, C), 1.0, 6.0, ((0, 16), (1, 16))),
        "filters": draw_filters(jax.random.fold_in(splits[3], 71), 0),
    }


def narrowed(values):
    return lax.optimization_barrier(values.astype(jnp.bfloat16))

def counting(length):
    return jnp.arange(length, dtype=jnp.int32)

def angle_table(row_index, col_index, modulus, direction):
    product = row_index[:, None] * col_index[None, :] % modulus
    angles = direction * 2.0 * math.pi / modulus * product.astype(jnp.float32)
    return (jnp.cos(angles), jnp.sin(angles))

def complex_block(cosine, sine_table):
    cos_half = narrowed(cosine).astype(jnp.float32)
    sin_half = narrowed(sine_table).astype(jnp.float32)
    return jnp.stack([jnp.stack([cos_half, -sin_half]), jnp.stack([sin_half, cos_half])])

def forward_whole(signal):
    signal_count, seq_total = signal.shape
    full_len = 2 * seq_total
    second_len = full_len // P_SIZE
    half_len = P_SIZE // 2
    shaped = signal.reshape(signal_count, half_len, second_len).astype(jnp.float32)
    cosine, sine_table = angle_table(counting(P_SIZE), counting(half_len), P_SIZE, -1.0)
    first_real = jnp.einsum('kn,mnq->mkq', narrowed(cosine).astype(jnp.float32), shaped)
    first_imag = jnp.einsum('kn,mnq->mkq', narrowed(sine_table).astype(jnp.float32), shaped)
    tw_cos, tw_sin = angle_table(counting(P_SIZE), counting(second_len), full_len, -1.0)
    second_real = narrowed(first_real * tw_cos - first_imag * tw_sin)
    second_imag = narrowed(first_real * tw_sin + first_imag * tw_cos)
    stacked = jnp.stack([second_real, second_imag]).astype(jnp.float32)
    cosine, sine_table = angle_table(counting(second_len), counting(second_len), second_len, -1.0)
    return narrowed(jnp.einsum('zwyq,wmkq->zmky', complex_block(cosine, sine_table), stacked))

def inverse_whole(spectrum):
    signal_count = spectrum.shape[1]
    second_len = spectrum.shape[3]
    full_len = P_SIZE * second_len
    half_len = P_SIZE // 2
    cosine, sine_table = angle_table(counting(second_len), counting(second_len), second_len, 1.0)
    first_pass = jnp.einsum('zwyq,wmkq->zmky', complex_block(cosine, sine_table), spectrum.astype(jnp.float32))
    tw_cos, tw_sin = angle_table(counting(P_SIZE), counting(second_len), full_len, 1.0)
    back_real = narrowed(first_pass[0] * tw_cos - first_pass[1] * tw_sin).astype(jnp.float32)
    back_imag = narrowed(first_pass[0] * tw_sin + first_pass[1] * tw_cos).astype(jnp.float32)
    cosine, sine_table = angle_table(counting(half_len), counting(P_SIZE), P_SIZE, 1.0)
    result = jnp.einsum('nk,mkq->mnq', narrowed(cosine).astype(jnp.float32), back_real)
    result = result - jnp.einsum('nk,mkq->mnq', narrowed(sine_table).astype(jnp.float32), back_imag)
    return (result * (1.0 / full_len)).reshape(signal_count, half_len * second_len)

def products(x_spec, dy_spec, h_spec):
    x_real = x_spec[0].astype(jnp.float32)
    x_imag = x_spec[1].astype(jnp.float32)
    dy_real = dy_spec[0].astype(jnp.float32)
    dy_imag = dy_spec[1].astype(jnp.float32)
    h_real = h_spec[0].astype(jnp.float32)
    h_imag = h_spec[1].astype(jnp.float32)
    y_spec = narrowed(jnp.stack([x_real * h_real - x_imag * h_imag, x_real * h_imag + x_imag * h_real]))
    dx_spec = narrowed(jnp.stack([dy_real * h_real + dy_imag * h_imag, dy_imag * h_real - dy_real * h_imag]))
    group_part = jnp.stack([dy_real * x_real + dy_imag * x_imag, dy_imag * x_real - dy_real * x_imag])
    return (y_spec, dx_spec, group_part)

def reference(seq_input, out_grad, filters):
    h_spec = forward_whole(filters.T)

    def one_block(accumulator, block_index):
        offset = (block_index * G).astype(jnp.int32)
        x_block = lax.dynamic_slice_in_dim(seq_input, offset, G, 1).T
        dy_block = lax.dynamic_slice_in_dim(out_grad, offset, G, 1).T
        spectra = forward_whole(jnp.concatenate([x_block, dy_block], axis=0))
        y_spec, dx_spec, group_part = products(spectra[:, :G], spectra[:, G:], h_spec)
        result = inverse_whole(jnp.concatenate([y_spec, dx_spec], axis=1)).astype(jnp.bfloat16)
        return (accumulator + group_part, (result[:G], result[G:]))
    accumulator = jnp.zeros((2, G, P_SIZE, Q), jnp.float32)
    group_spec, outs = lax.scan(one_block, accumulator, jnp.arange(N_CH, dtype=jnp.int32))
    conv_out = outs[0].transpose(2, 0, 1).reshape(TOKENS, C)
    input_grad = outs[1].transpose(2, 0, 1).reshape(TOKENS, C)
    filter_grad = (inverse_whole(narrowed(group_spec)) * (1.0 / math.sqrt(TOKENS * N_CH))).T
    return (conv_out, input_grad, filter_grad)
```

```python
import functools
import math

import jax
import jax.numpy as jnp
import numpy as np
from jax import lax
from jax.experimental import pallas as pl
from jax.experimental.pallas import tpu as pltpu
from jax.sharding import Mesh
from jax.sharding import PartitionSpec as P

BF = jnp.bfloat16
F32 = jnp.float32
FACTOR = 256
HALF = 128
FULL = FACTOR * FACTOR
CTX = 16
SUB = HALF // CTX
TOK = SUB * FACTOR
COLS = 8
ZH = 4
Y = 4
GRAD_SCALE = 1.0 / math.sqrt(524288)


def unit(product, modulus):
    angles = np.float32(2.0 * math.pi / modulus) * (product % modulus).astype(np.float32)
    return np.cos(angles).astype(np.float32), np.sin(angles).astype(np.float32)


def tables():
    row = np.arange(HALF)
    n1 = (row % CTX) * SUB + row // CTX
    k1 = np.arange(HALF)
    n2 = np.arange(FACTOR)
    cos1, sin1 = unit((2 * k1[:, None] + 1) * n1[None, :], 2 * FACTOR)
    cos2, sin2 = unit(n2[:, None] * n2[None, :], FACTOR)
    tw_cos, tw_sin = unit((2 * k1[:, None] + 1) * n2[None, :], 2 * FULL)
    first = np.concatenate([cos1, -sin1], 0)
    second = np.block([[cos2, -sin2], [sin2, cos2]])
    back_first = np.block([[cos2, sin2], [-sin2, cos2]])
    back_last = np.concatenate([cos1.T, -sin1.T], 1) * np.float32(2.0 / FULL)
    half = lambda a: jnp.asarray(a, dtype=BF)
    return half(first), half(second), half(back_first), half(back_last), jnp.asarray(tw_cos), jnp.asarray(tw_sin)


def mm(a, b):
    return jnp.dot(a, b, preferred_element_type=F32)


def column(rows):
    return jnp.concatenate([rows[:, k * FACTOR : (k + 1) * FACTOR] for k in range(SUB)], axis=0)


def flat(block):
    return jnp.concatenate([block[k * CTX : (k + 1) * CTX] for k in range(SUB)], axis=1)


def permute_rows(dst, perm, src):
    step = 512
    for at in range(0, TOK, step):
        dst[:, at : at + step] = mm(perm[...], src[:, at : at + step]).astype(BF)


def twist(first, cos, sin):
    real, imag = first[:HALF], first[HALF:]
    return jnp.concatenate([real * cos + imag * sin, imag * cos - real * sin], axis=1).astype(BF)


def untwist(first, cos, sin):
    real, imag = first[:, :FACTOR], first[:, FACTOR:]
    return jnp.concatenate([real * cos - imag * sin, real * sin + imag * cos], axis=0).astype(BF)


def split(spec):
    return spec[:, :FACTOR].astype(F32), spec[:, FACTOR:].astype(F32)


def spread_kernel(x_ref, dy_ref, f_ref, perm_ref, eye_ref, out_ref, taps_ref):
    nt = (((1,), (1,)), ((), ()))
    step = 512
    for at in range(0, TOK, step):
        both = jnp.concatenate([x_ref[at : at + step], dy_ref[at : at + step]], axis=1)
        out_ref[:, at : at + step] = lax.dot_general(perm_ref[...], both, nt, preferred_element_type=F32).astype(BF)
    taps_ref[...] = lax.dot_general(eye_ref[...], f_ref[...], nt, preferred_element_type=F32).astype(BF)


def filter_kernel(r_ref, perm_ref, t1_ref, t2_ref, cos_ref, sin_ref, spec_ref, rp_ref):
    permute_rows(rp_ref, perm_ref, r_ref)

    def body(at, carry):
        cos, sin = cos_ref[...], sin_ref[...]
        parts = []
        for k in range(2):
            rows = rp_ref[pl.ds(pl.multiple_of((at * 2 + k) * CTX, CTX), CTX), :]
            parts.append(column(rows))
        first = mm(t1_ref[...], jnp.concatenate(parts, axis=1))
        second = jnp.concatenate([twist(first[:, k * FACTOR : (k + 1) * FACTOR], cos, sin) for k in range(2)], axis=0)
        spec = mm(second, t2_ref[...]).astype(BF)
        for k in range(2):
            spec_ref[at * 2 + k] = spec[k * HALF : (k + 1) * HALF]
        return carry

    lax.fori_loop(0, COLS // 2, body, 0)


def forward_kernel(r_ref, perm_ref, gperm_ref, t1_ref, t2_ref, t2i_ref, t1i_ref, cos_ref, sin_ref, spec_ref, g_ref, rp_ref, gs_ref):
    permute_rows(rp_ref, perm_ref, r_ref)

    def body(c, carry):
        cos, sin = cos_ref[...], sin_ref[...]
        parts = []
        for s in range(2):
            rows = rp_ref[pl.ds(pl.multiple_of(s * HALF + c * CTX, CTX), CTX), :]
            parts.append(column(rows))
        first = mm(t1_ref[...], jnp.concatenate(parts, axis=1))
        second = jnp.concatenate([twist(first[:, k * FACTOR : (k + 1) * FACTOR], cos, sin) for k in range(2)], axis=0)
        spec = mm(second, t2_ref[...])
        spec_ref[c] = spec.astype(BF)
        x_real, x_imag = split(spec[:HALF])
        dy_real, dy_imag = split(spec[HALF:])
        group = jnp.concatenate(
            [dy_real * x_real + dy_imag * x_imag, dy_imag * x_real - dy_real * x_imag], axis=1
        ).astype(BF)
        back = untwist(mm(group, t2i_ref[...]), cos, sin)
        out = mm(t1i_ref[...], back) * GRAD_SCALE
        gs_ref[pl.ds(pl.multiple_of(c * CTX, CTX), CTX), :] = flat(out.astype(BF))
        return carry

    lax.fori_loop(0, COLS, body, 0)
    permute_rows(g_ref, gperm_ref, gs_ref)


def backward_kernel(spec_ref, h_ref, perm_ref, t2i_ref, t1i_ref, cos_ref, sin_ref, out_ref, os_ref):
    def body(c, carry):
        cos, sin = cos_ref[...], sin_ref[...]
        spec = spec_ref[c]
        x_real, x_imag = split(spec[:HALF])
        dy_real, dy_imag = split(spec[HALF:])
        h_real, h_imag = split(h_ref[c])
        y = jnp.concatenate([x_real * h_real - x_imag * h_imag, x_real * h_imag + x_imag * h_real], axis=1)
        dx = jnp.concatenate([dy_real * h_real + dy_imag * h_imag, dy_imag * h_real - dy_real * h_imag], axis=1)
        both = jnp.concatenate([y.astype(BF), dx.astype(BF)], axis=0)
        first = mm(both, t2i_ref[...])
        back = jnp.concatenate([untwist(first[s * HALF : (s + 1) * HALF], cos, sin) for s in range(2)], axis=1)
        out = mm(t1i_ref[...], back).astype(BF)
        for s in range(2):
            at = pl.multiple_of(s * HALF + c * CTX, CTX)
            os_ref[pl.ds(at, CTX), :] = flat(out[:, s * FACTOR : (s + 1) * FACTOR])
        return carry

    lax.fori_loop(0, COLS, body, 0)
    permute_rows(out_ref, perm_ref, os_ref)


def place_kernel(r_ref, perm_ref, a_ref, b_ref):
    tn = (((0,), (0,)), ((), ()))
    step = 512
    for at in range(0, TOK, step):
        both = lax.dot_general(r_ref[:, at : at + step], perm_ref[...], tn, preferred_element_type=F32).astype(BF)
        a_ref[at : at + step] = both[:, :HALF]
        b_ref[at : at + step] = both[:, HALF:]


def grad_kernel(r_ref, perm_ref, out_ref):
    tn = (((0,), (0,)), ((), ()))
    step = 512
    for at in range(0, TOK, step):
        out_ref[at : at + step] = lax.dot_general(r_ref[:, at : at + step], perm_ref[...], tn, preferred_element_type=F32)


def call(kernel, outs, scratch, flops, moved, *args):
    return pl.pallas_call(
        kernel,
        out_shape=[jax.ShapeDtypeStruct(*o) for o in outs],
        scratch_shapes=[pltpu.VMEM(*s) for s in scratch],
        compiler_params=pltpu.CompilerParams(vmem_limit_bytes=40 * 1024 * 1024),
        cost_estimate=pl.CostEstimate(flops=flops, bytes_accessed=moved, transcendentals=0),
    )(*args)


def one_hot(index, count):
    out = np.zeros((len(index), count), np.float32)
    out[np.arange(len(index)), index] = 1.0
    return jnp.asarray(out, dtype=BF)


def rows_of(*sizes):
    return np.unravel_index(np.arange(int(np.prod(sizes))), sizes)


def spread_perm():
    d, s, c = rows_of(CTX, 2, COLS)
    return one_hot(s * HALF + d * COLS + c, 2 * HALF)


def arrive_perm():
    s, c, d = rows_of(2, COLS, CTX)
    return one_hot(d * 2 * COLS + s * COLS + c, 2 * HALF)


def leave_perm():
    d, s, c = rows_of(CTX, 2, COLS)
    return one_hot(s * HALF + c * CTX + d, 2 * HALF)


def place_perm():
    d, s, c = rows_of(CTX, 2, COLS)
    return one_hot(s * HALF + d * COLS + c, 2 * HALF)


def relative(sign, my_zh, my_y):
    ky, kzh, c = rows_of(Y, ZH, COLS)
    block = (my_zh + sign * kzh) % ZH * Y + (my_y + sign * ky) % Y
    return block, c


def hot(index):
    return (index[:, None] == jnp.arange(HALF)[None, :]).astype(BF)


def shifted(x, axis, size, k):
    return lax.ppermute(x, axis, [(s, (s + k) % size) for s in range(size)])


def swap(x):
    return lax.ppermute(x, ("ctx", "zh", "y"), [(a * CTX + b, b * CTX + a) for a in range(CTX) for b in range(CTX)])


def gather(x):
    rows = x.shape[0]
    x = jnp.concatenate([x] + [shifted(x, "zh", ZH, k) for k in range(1, ZH)], axis=0)
    return jnp.concatenate([x] + [shifted(x, "y", Y, k) for k in range(1, Y)], axis=0)


def scatter_sum(x):
    for axis, size in (("y", Y), ("zh", ZH)):
        rows = x.shape[0] // size
        parts = [x[:rows]] + [shifted(x[k * rows : (k + 1) * rows], axis, size, k) for k in range(1, size)]
        x = sum(p.astype(F32) for p in parts).astype(BF)
    return x


def local(seq_input, out_grad, filters):
    first, second, back_first, back_last, tw_cos, tw_sin = tables()
    my_zh, my_y = lax.axis_index("zh"), lax.axis_index("y")
    come, c = relative(-1, my_zh, my_y)
    go, _ = relative(1, my_zh, my_y)
    filter_perm = hot(c * CTX + come).T
    leave_grad = hot(c * CTX + go)
    place_grad = hot(come * COLS + c)

    spread, taps = call(
        spread_kernel,
        [((2 * HALF, TOK), BF), ((COLS, TOK), BF)],
        [],
        2 * 256 * 256 * 2048,
        3 << 20,
        seq_input,
        out_grad,
        filters,
        spread_perm(),
        jnp.eye(COLS, dtype=BF),
    )
    arrived = lax.all_to_all(spread.reshape(CTX, 2 * COLS, TOK), "ctx", 0, 0, tiled=True).reshape(2 * HALF, TOK)
    taps = gather(swap(taps))
    (h_spec,) = call(
        filter_kernel,
        [((COLS, HALF, 2 * FACTOR), BF)],
        [((HALF, TOK), BF)],
        2 * 8 * 42 * 10**6,
        3 << 20,
        taps,
        filter_perm,
        first,
        second,
        tw_cos,
        tw_sin,
    )
    spec, grads = call(
        forward_kernel,
        [((COLS, 2 * HALF, 2 * FACTOR), BF), ((HALF, TOK), BF)],
        [((2 * HALF, TOK), BF), ((HALF, TOK), BF)],
        2 * 24 * 42 * 10**6,
        6 << 20,
        arrived,
        arrive_perm(),
        leave_grad,
        first,
        second,
        back_first,
        back_last,
        tw_cos,
        tw_sin,
    )
    (leaving,) = call(
        backward_kernel,
        [((2 * HALF, TOK), BF)],
        [((2 * HALF, TOK), BF)],
        2 * 16 * 42 * 10**6,
        6 << 20,
        spec,
        h_spec,
        leave_perm(),
        back_first,
        back_last,
        tw_cos,
        tw_sin,
    )
    back = lax.all_to_all(leaving.reshape(CTX, 2 * COLS, TOK), "ctx", 0, 0, tiled=True).reshape(2 * HALF, TOK)
    grads = gather(swap(scatter_sum(grads)))
    conv_out, input_grad = call(
        place_kernel,
        [((TOK, HALF), BF), ((TOK, HALF), BF)],
        [],
        2 * 256 * 256 * 2048,
        2 << 20,
        back,
        place_perm(),
    )
    (filter_grad,) = call(
        grad_kernel, [((TOK, HALF), F32)], [], 2 * 128 * 128 * 2048, 2 << 20, grads, place_grad
    )
    return conv_out, input_grad, filter_grad


def solution(mesh):
    inner = Mesh(mesh.devices.reshape(CTX, ZH, Y), ("ctx", "zh", "y"))
    placed = P("ctx", ("zh", "y"))
    return jax.shard_map(
        local,
        mesh=inner,
        in_specs=(placed, placed, placed),
        out_specs=(placed, placed, P("ctx", None)),
        check_vma=False,
    )
```

```python
import math

import jax
import jax.numpy as jnp
import numpy as np
from jax import lax
from jax.experimental import pallas as pl
from jax.experimental.pallas import tpu as pltpu
from jax.sharding import Mesh
from jax.sharding import PartitionSpec as P

BF = jnp.bfloat16
F32 = jnp.float32
FACTOR = 256
HALF = 128
FULL = FACTOR * FACTOR
CTX = 16
SUB = HALF // CTX
TOK = SUB * FACTOR
COLS = 8
PAIR = 2
ZH = 4
Y = 4
STEP = 512
LARGE = 60 * 1024 * 1024
GRAD_SCALE = 1.0 / math.sqrt(524288)


def unit(product, modulus):
    angles = np.float32(2.0 * math.pi / modulus) * (product % modulus).astype(np.float32)
    return np.cos(angles).astype(np.float32), np.sin(angles).astype(np.float32)


def tables():
    row = np.arange(HALF)
    n1 = (row % CTX) * SUB + row // CTX
    k1 = np.arange(HALF)
    n2 = np.arange(FACTOR)
    cos1, sin1 = unit((2 * k1[:, None] + 1) * n1[None, :], 2 * FACTOR)
    cos2, sin2 = unit(n2[:, None] * n2[None, :], FACTOR)
    tw_cos, tw_sin = unit((2 * k1[:, None] + 1) * n2[None, :], 2 * FULL)
    first = np.concatenate([cos1, -sin1], 0)
    second = np.block([[cos2, -sin2], [sin2, cos2]])
    back_last = np.concatenate([cos1.T, -sin1.T], 1) * np.float32(2.0 / FULL)
    back_plain = back_last.reshape(SUB, CTX, FACTOR).transpose(1, 0, 2).reshape(HALF, FACTOR)
    half = lambda a: jnp.asarray(a, dtype=BF)
    return half(first), half(second), half(back_last), half(back_plain), jnp.asarray(tw_cos), jnp.asarray(tw_sin)


def mm(a, b):
    return jnp.dot(a, b, preferred_element_type=F32)


def column(rows):
    return jnp.concatenate([rows[:, k * FACTOR : (k + 1) * FACTOR] for k in range(SUB)], axis=0)


def flat(block):
    return jnp.concatenate([block[k * CTX : (k + 1) * CTX] for k in range(SUB)], axis=1)


def permute_rows(dst, perm, src):
    for at in range(0, TOK, STEP):
        dst[:, at : at + STEP] = mm(perm, src[:, at : at + STEP]).astype(BF)


def sends(row_of):
    row = lax.broadcasted_iota(jnp.int32, (FACTOR, FACTOR), 0)
    col = lax.broadcasted_iota(jnp.int32, (FACTOR, FACTOR), 1)
    return (col == row_of(row)).astype(F32).astype(BF)


def by_block(r):
    return ((r >> 3) & 1) * HALF + (r >> 4) * COLS + (r & 7)


def turned(r):
    return (r & 15) * CTX + (r >> 4)


def to_subs(r):
    return (r & 31) * SUB + (r >> 5)


def twist(first, cos, sin):
    real, imag = first[:HALF], first[HALF:]
    return jnp.concatenate([real * cos + imag * sin, imag * cos - real * sin], axis=1).astype(BF)


def untwist(first, cos, sin):
    real, imag = first[:, :FACTOR], first[:, FACTOR:]
    return jnp.concatenate([real * cos + imag * sin, real * sin - imag * cos], axis=0).astype(BF)


def split(spec):
    return spec[:, :FACTOR].astype(F32), spec[:, FACTOR:].astype(F32)


def spread_kernel(x_ref, dy_ref, out_ref, held, put, in_sems, out_sems):
    nt = (((1,), (1,)), ((), ()))
    chunks = [pl.ds(at, STEP) for at in range(0, TOK, STEP)]
    takes = []
    for k, chunk in enumerate(chunks):
        for s, ref in enumerate((x_ref, dy_ref)):
            take = pltpu.make_async_copy(
                ref.at[chunk], held.at[chunk, pl.ds(s * HALF, HALF)], in_sems.at[2 * k + s]
            )
            take.start()
            takes.append(take)
    perm = sends(by_block)
    gives = []
    for k, chunk in enumerate(chunks):
        takes[2 * k].wait()
        takes[2 * k + 1].wait()
        put[:, chunk] = lax.dot_general(perm, held[chunk], nt, preferred_element_type=F32).astype(BF)
        give = pltpu.make_async_copy(put.at[:, chunk], out_ref.at[:, chunk], out_sems.at[k])
        give.start()
        gives.append(give)
    for give in gives:
        give.wait()


def filter_kernel(a_ref, b_ref, c_ref, d_ref, perm_ref, t1_ref, t2_ref, cos_ref, sin_ref, spec_ref, rp_ref):
    permute_rows(rp_ref, perm_ref[...], jnp.concatenate([r[...] for r in (a_ref, b_ref, c_ref, d_ref)], axis=0))

    def body(at, carry):
        cos, sin = cos_ref[...], sin_ref[...]
        parts = []
        for k in range(4):
            rows = rp_ref[pl.ds(pl.multiple_of((at * 4 + k) * CTX, CTX), CTX), :]
            parts.append(column(rows))
        first = mm(t1_ref[...], jnp.concatenate(parts, axis=1))
        second = jnp.concatenate([twist(first[:, k * FACTOR : (k + 1) * FACTOR], cos, sin) for k in range(4)], axis=0)
        spec = mm(second, t2_ref[...]).astype(BF)
        for k in range(4):
            spec_ref[at * 4 + k] = spec[k * HALF : (k + 1) * HALF]
        return carry

    lax.fori_loop(0, COLS // 4, body, 0)


def forward_kernel(r_ref, t1_ref, t2_ref, t1g_ref, cos_ref, sin_ref, spec_ref, g_ref, rp_ref):
    permute_rows(rp_ref, sends(turned), r_ref)

    def body(pair, carry):
        cos, sin = cos_ref[...], sin_ref[...]
        parts = []
        for k in range(PAIR):
            for s in range(2):
                at = pl.multiple_of(s * HALF + (pair * PAIR + k) * CTX, CTX)
                parts.append(column(rp_ref[pl.ds(at, CTX), :]))
        first = mm(t1_ref[...], jnp.concatenate(parts, axis=1))
        second = jnp.concatenate(
            [twist(first[:, k * FACTOR : (k + 1) * FACTOR], cos, sin) for k in range(2 * PAIR)], axis=0
        )
        spec = mm(second, t2_ref[...])
        groups = []
        for k in range(PAIR):
            both = spec[k * 2 * HALF : (k + 1) * 2 * HALF]
            spec_ref[pair * PAIR + k] = both.astype(BF)
            x_real, x_imag = split(both[:HALF])
            dy_real, dy_imag = split(both[HALF:])
            groups.append(
                jnp.concatenate(
                    [dy_real * x_real + dy_imag * x_imag, dy_real * x_imag - dy_imag * x_real], axis=1
                ).astype(BF)
            )
        back = mm(jnp.concatenate(groups, axis=0), t2_ref[...])
        back = jnp.concatenate([untwist(back[k * HALF : (k + 1) * HALF], cos, sin) for k in range(PAIR)], axis=1)
        out = mm(t1g_ref[...], back) * GRAD_SCALE
        for d in range(CTX):
            rows = [out[d * SUB : (d + 1) * SUB, k * FACTOR : (k + 1) * FACTOR] for k in range(PAIR)]
            g_ref[d * Y + pair] = jnp.concatenate(rows, axis=0).astype(BF)
        return carry

    lax.fori_loop(0, COLS // PAIR, body, 0)


def backward_kernel(spec_ref, h_ref, t2_ref, t1i_ref, cos_ref, sin_ref, out_ref, os_ref):
    def body(pair, carry):
        cos, sin = cos_ref[...], sin_ref[...]
        parts = []
        for k in range(PAIR):
            spec = spec_ref[pair * PAIR + k]
            x_real, x_imag = split(spec[:HALF])
            dy_real, dy_imag = split(spec[HALF:])
            h_real, h_imag = split(h_ref[pair * PAIR + k])
            y = [x_real * h_real - x_imag * h_imag, -(x_real * h_imag + x_imag * h_real)]
            dx = [dy_real * h_real + dy_imag * h_imag, dy_real * h_imag - dy_imag * h_real]
            parts += [jnp.concatenate(y, axis=1).astype(BF), jnp.concatenate(dx, axis=1).astype(BF)]
        first = mm(jnp.concatenate(parts, axis=0), t2_ref[...])
        back = jnp.concatenate(
            [untwist(first[k * HALF : (k + 1) * HALF], cos, sin) for k in range(2 * PAIR)], axis=1
        )
        out = mm(t1i_ref[...], back).astype(BF)
        for k in range(PAIR):
            for s in range(2):
                at = pl.multiple_of(s * HALF + (pair * PAIR + k) * CTX, CTX)
                lane = (2 * k + s) * FACTOR
                os_ref[pl.ds(at, CTX), :] = flat(out[:, lane : lane + FACTOR])
        return carry

    lax.fori_loop(0, COLS // PAIR, body, 0)
    permute_rows(out_ref, sends(turned), os_ref)


def place_kernel(r_ref, a_ref, b_ref, put, sems):
    tn = (((0,), (0,)), ((), ()))
    perm = sends(by_block)
    gives = []
    for k in range(TOK // STEP):
        chunk = pl.ds(k * STEP, STEP)
        both = lax.dot_general(r_ref[:, k * STEP : (k + 1) * STEP], perm, tn, preferred_element_type=F32).astype(BF)
        for s, ref in enumerate((a_ref, b_ref)):
            put[s, chunk] = both[:, s * HALF : (s + 1) * HALF]
            give = pltpu.make_async_copy(put.at[s, chunk], ref.at[chunk], sems.at[2 * k + s])
            give.start()
            gives.append(give)
    for give in gives:
        give.wait()


def grad_kernel(a_ref, b_ref, c_ref, d_ref, perm_ref, out_ref, put, sems):
    tn = (((0,), (0,)), ((), ()))
    sort = sends(to_subs)
    blocks = [mm(sort, r[...]).astype(BF) for r in (a_ref, b_ref, c_ref, d_ref)]
    rows = CTX * PAIR
    gives = []
    for n in range(SUB):
        chunk = pl.ds(n * FACTOR, FACTOR)
        part = jnp.concatenate([block[n * rows : (n + 1) * rows] for block in blocks], axis=0)
        put[chunk] = lax.dot_general(part, perm_ref[...], tn, preferred_element_type=F32)
        give = pltpu.make_async_copy(put.at[chunk], out_ref.at[chunk], sems.at[n])
        give.start()
        gives.append(give)
    for give in gives:
        give.wait()


def call(kernel, outs, scratch, flops, moved, *args, ins=None, space=pltpu.VMEM, limit=40 * 1024 * 1024):
    return pl.pallas_call(
        kernel,
        in_specs=[pl.BlockSpec(memory_space=ins or pltpu.VMEM)] * len(args),
        out_specs=[pl.BlockSpec(memory_space=space)] * len(outs),
        out_shape=[jax.ShapeDtypeStruct(*o) for o in outs],
        scratch_shapes=scratch,
        compiler_params=pltpu.CompilerParams(vmem_limit_bytes=limit),
        cost_estimate=pl.CostEstimate(flops=flops, bytes_accessed=moved, transcendentals=0),
    )(*args)


def rows_of(*sizes):
    return np.unravel_index(np.arange(int(np.prod(sizes))), sizes)


def hot(index):
    return (index[:, None] == jnp.arange(HALF)[None, :]).astype(BF)


def shifted(x, axis, size, k):
    return lax.ppermute(x, axis, [(s, (s + k) % size) for s in range(size)])


def swap(x):
    return lax.ppermute(x, ("ctx", "zh", "y"), [(a * CTX + b, b * CTX + a) for a in range(CTX) for b in range(CTX)])


def arrivals(x, axis, size):
    return [x] + [shifted(x, axis, size, k) for k in range(1, size)]


def added(parts):
    a, b, c, d = (p.astype(F32) for p in parts)
    return ((a + c) + (b + d)).astype(BF)


def local(seq_input, out_grad, filters):
    first, second, back_last, back_plain, tw_cos, tw_sin = tables()
    my_zh, my_y = lax.axis_index("zh"), lax.axis_index("y")
    ky, kzh, c = rows_of(Y, ZH, COLS)
    filter_perm = hot(c * CTX + (my_zh - kzh) % ZH * Y + (my_y - ky) % Y).T
    ky, i, c = rows_of(Y, CTX, PAIR)
    place_grad = hot(i * COLS + (my_y - ky) % Y * PAIR + c)

    taps = swap(filters.T)
    (spread,) = call(
        spread_kernel,
        [((FACTOR, TOK), BF)],
        [
            pltpu.VMEM((TOK, FACTOR), BF),
            pltpu.VMEM((FACTOR, TOK), BF),
            pltpu.SemaphoreType.DMA((2 * TOK // STEP,)),
            pltpu.SemaphoreType.DMA((TOK // STEP,)),
        ],
        2 * 256 * 256 * 2048,
        2 << 20,
        seq_input,
        out_grad,
        ins=pl.ANY,
        space=pl.ANY,
        limit=LARGE,
    )
    arrived = lax.all_to_all(spread.reshape(CTX, 2 * COLS, TOK), "ctx", 0, 0, tiled=True).reshape(2 * HALF, TOK)
    spec, grads = call(
        forward_kernel,
        [((COLS, 2 * HALF, 2 * FACTOR), BF), ((CTX * Y, CTX, FACTOR), BF)],
        [pltpu.VMEM((2 * HALF, TOK), BF)],
        2 * 24 * 42 * 10**6,
        6 << 20,
        arrived,
        first,
        second,
        back_plain,
        tw_cos,
        tw_sin,
    )
    spec, grads, taps = lax.optimization_barrier((spec, grads, taps))
    taps = arrivals(taps, "zh", ZH)
    taps = arrivals(jnp.concatenate(taps, axis=0), "y", Y)
    (h_spec,) = call(
        filter_kernel,
        [((COLS, HALF, 2 * FACTOR), BF)],
        [pltpu.VMEM((HALF, TOK), BF)],
        2 * 8 * 42 * 10**6,
        3 << 20,
        *taps,
        filter_perm,
        first,
        second,
        tw_cos,
        tw_sin,
    )
    grads = lax.all_to_all(grads, ("ctx", "y"), 0, 0, tiled=True).reshape(CTX, Y, CTX, FACTOR)
    grads = jnp.sum(grads.astype(F32), axis=1).astype(BF).reshape(FACTOR, FACTOR)
    (leaving,) = call(
        backward_kernel,
        [((2 * HALF, TOK), BF)],
        [pltpu.VMEM((2 * HALF, TOK), BF)],
        2 * 16 * 42 * 10**6,
        6 << 20,
        spec,
        h_spec,
        second,
        back_last,
        tw_cos,
        tw_sin,
    )
    grads = added(arrivals(grads, "zh", ZH))
    grads, leaving = lax.optimization_barrier((grads, leaving))
    back = lax.all_to_all(leaving.reshape(CTX, 2 * COLS, TOK), "ctx", 0, 0, tiled=True).reshape(2 * HALF, TOK)
    grads = arrivals(grads, "y", Y)
    conv_out, input_grad = call(
        place_kernel,
        [((TOK, HALF), BF), ((TOK, HALF), BF)],
        [pltpu.VMEM((2, TOK, HALF), BF), pltpu.SemaphoreType.DMA((2 * TOK // STEP,))],
        2 * 256 * 256 * 2048,
        2 << 20,
        back,
        space=pl.ANY,
    )
    (filter_grad,) = call(
        grad_kernel,
        [((TOK, HALF), F32)],
        [pltpu.VMEM((TOK, HALF), F32), pltpu.SemaphoreType.DMA((SUB,))],
        2 * 256 * 256 * 1024,
        2 << 20,
        *grads,
        place_grad,
        space=pl.ANY,
    )
    return conv_out, input_grad, filter_grad


def solution(mesh):
    inner = Mesh(mesh.devices.reshape(CTX, ZH, Y), ("ctx", "zh", "y"))
    placed = P("ctx", ("zh", "y"))
    return jax.shard_map(
        local,
        mesh=inner,
        in_specs=(placed, placed, placed),
        out_specs=(placed, placed, P("ctx", None)),
        check_vma=False,
    )
```

```python
import math

import jax
import jax.numpy as jnp
import numpy as np
from jax import lax
from jax.experimental import pallas as pl
from jax.experimental.pallas import tpu as pltpu
from jax.sharding import Mesh
from jax.sharding import PartitionSpec as P

BF = jnp.bfloat16
F32 = jnp.float32
FACTOR = 256
HALF = 128
FULL = FACTOR * FACTOR
CTX = 16
SUB = HALF // CTX
TOK = SUB * FACTOR
PAIR = 2
ZH = 4
Y = 4
LARGE = 60 * 1024 * 1024
GRAD_SCALE = 1.0 / math.sqrt(524288)


def unit(product, modulus):
    angles = np.float32(2.0 * math.pi / modulus) * (product % modulus).astype(np.float32)
    return np.cos(angles).astype(np.float32), np.sin(angles).astype(np.float32)


def tables():
    n1 = np.arange(HALF)
    k1 = np.arange(HALF)
    n2 = np.arange(FACTOR)
    cos1, sin1 = unit((2 * k1[:, None] + 1) * n1[None, :], 2 * FACTOR)
    cos2, sin2 = unit(n2[:, None] * n2[None, :], FACTOR)
    tw_cos, tw_sin = unit((2 * k1[:, None] + 1) * n2[None, :], 2 * FULL)
    first = np.concatenate([cos1, -sin1], 0)
    second = np.block([[cos2, -sin2], [sin2, cos2]])
    back_last = np.concatenate([cos1.T, -sin1.T], 1) * np.float32(2.0 / FULL)
    half = lambda a: jnp.asarray(a, dtype=BF)
    return half(first), half(second), half(back_last), jnp.asarray(tw_cos), jnp.asarray(tw_sin)


def mm(a, b):
    return jnp.dot(a, b, preferred_element_type=F32)


def ones_at(row_of, size=FACTOR):
    row = lax.broadcasted_iota(jnp.int32, (size, size), 0)
    col = lax.broadcasted_iota(jnp.int32, (size, size), 1)
    return (col == row_of(row)).astype(F32).astype(BF)


def to_owners(r):
    return (r & 7) * 32 + ((r >> 4) & 1) * 16 + (r >> 5) * PAIR + ((r >> 3) & 1)


def to_subs(r):
    return ((r >> 1) & 7) * 32 + ((r >> 4) & 1) * 16 + (r & 1) * 8 + (r >> 5)


def subs_first(r):
    return (r & 31) * SUB + (r >> 5)


def twist(first, cos, sin):
    real, imag = first[:HALF], first[HALF:]
    return jnp.concatenate([real * cos + imag * sin, imag * cos - real * sin], axis=1).astype(BF)


def untwist(first, cos, sin):
    real, imag = first[:, :FACTOR], first[:, FACTOR:]
    return jnp.concatenate([real * cos + imag * sin, real * sin - imag * cos], axis=0).astype(BF)


def split(spec):
    return spec[:, :FACTOR].astype(F32), spec[:, FACTOR:].astype(F32)


def forward(columns, t1, t2, cos, sin):
    first = mm(t1, jnp.concatenate(columns, axis=1))
    count = len(columns)
    second = [twist(first[:, k * FACTOR : (k + 1) * FACTOR], cos, sin) for k in range(count)]
    return mm(jnp.concatenate(second, axis=0), t2)


def backward(spectra, t2, t1i, cos, sin):
    first = mm(jnp.concatenate(spectra, axis=0), t2)
    count = len(spectra)
    back = [untwist(first[k * HALF : (k + 1) * HALF], cos, sin) for k in range(count)]
    return mm(t1i, jnp.concatenate(back, axis=1))


def spread_kernel(x_ref, dy_ref, out_ref, held, put, in_sems, out_sems):
    takes = []
    for n in range(SUB):
        chunk = pl.ds(n * FACTOR, FACTOR)
        for s, ref in enumerate((x_ref, dy_ref)):
            take = pltpu.make_async_copy(
                ref.at[chunk], held.at[s, chunk], in_sems.at[2 * n + s]
            )
            take.start()
            takes.append(take)
    sort = ones_at(to_owners)
    turned = []
    for n in range(SUB):
        takes[2 * n].wait()
        takes[2 * n + 1].wait()
        turned.append([held[s, n * FACTOR : (n + 1) * FACTOR].T for s in range(2)])
    gives = []
    for g in range(SUB):
        chunk = pl.ds(g * SUB, SUB)
        rows = jnp.concatenate([t[g * 16 : (g + 1) * 16] for pair in turned for t in pair], axis=0)
        rows = mm(sort, rows).astype(BF)
        for k in range(2):
            put[chunk, 32 * k : 32 * (k + 1)] = rows[:, k * HALF : (k + 1) * HALF].reshape(SUB, 32, HALF)
        give = pltpu.make_async_copy(put.at[chunk], out_ref.at[chunk], out_sems.at[g])
        give.start()
        gives.append(give)
    for give in gives:
        give.wait()


def forward_kernel(r_ref, t1_ref, t2_ref, t1i_ref, cos_ref, sin_ref, spec_ref, g_ref, acc_ref):
    acc_ref[...] = jnp.zeros_like(acc_ref)

    def body(j):
        tiles = [
            jnp.concatenate([r_ref[i * Y + j, :32], r_ref[i * Y + j, 32:]], axis=1).astype(F32) for i in range(CTX)
        ]
        columns = [
            jnp.concatenate([t[q * SUB : (q + 1) * SUB] for t in tiles], axis=0).astype(BF) for q in range(4)
        ]
        spec = forward(columns, t1_ref[...], t2_ref[...], cos_ref[...], sin_ref[...])
        spec_ref[j] = spec.astype(BF)
        for f in range(PAIR):
            x_real, x_imag = split(spec[f * HALF : (f + 1) * HALF])
            dy_real, dy_imag = split(spec[(PAIR + f) * HALF : (PAIR + f + 1) * HALF])
            acc_ref[f] += jnp.concatenate(
                [dy_real * x_real + dy_imag * x_imag, dy_real * x_imag - dy_imag * x_real], axis=1
            )

    for j in range(Y):
        body(j)
    groups = [acc_ref[f].astype(BF) for f in range(PAIR)]
    out = backward(groups, t2_ref[...], t1i_ref[...], cos_ref[...], sin_ref[...]) * GRAD_SCALE
    for d in range(CTX):
        rows = [out[d * SUB : (d + 1) * SUB, f * FACTOR : (f + 1) * FACTOR] for f in range(PAIR)]
        g_ref[d] = jnp.concatenate(rows, axis=0).astype(BF)


def pack_kernel(part_ref, a_ref, b_ref, out_ref):
    out_ref[:CTX] = part_ref[...]
    out_ref[CTX : CTX + 2] = a_ref[...]
    out_ref[CTX + 2 :] = b_ref[...]


def backward_kernel(
    spec_ref, all_ref, me_ref, t1_ref, t2_ref, t1i_ref, cos_ref, sin_ref, out_ref, h_ref
):
    my_y = me_ref[0]
    parts = [all_ref.at[z] for z in range(ZH)]

    def arrival(r):
        block = r >> 3
        return ((block >> 2 << 2) + ((block & 3) ^ my_y)) * SUB + (r & 7)

    order = ones_at(arrival, HALF)
    tiles = [ref[CTX + k].astype(F32) for ref in parts for k in range(Y)]
    taps = [jnp.concatenate([t[f * SUB : (f + 1) * SUB] for t in tiles], axis=0).astype(BF) for f in range(PAIR)]
    taps = mm(order, jnp.concatenate(taps, axis=1)).astype(BF)
    columns = [taps[:, f * FACTOR : (f + 1) * FACTOR] for f in range(PAIR)]
    h_ref[...] = forward(columns, t1_ref[...], t2_ref[...], cos_ref[...], sin_ref[...])

    def body(j):
        spectra = []
        for s in range(2):
            for f in range(PAIR):
                at = (s * PAIR + f) * HALF
                real, imag = split(spec_ref[j, at : at + HALF])
                h_real, h_imag = split(h_ref[f * HALF : (f + 1) * HALF])
                if s == 0:
                    both = [real * h_real - imag * h_imag, -(real * h_imag + imag * h_real)]
                else:
                    both = [real * h_real + imag * h_imag, real * h_imag - imag * h_real]
                spectra.append(jnp.concatenate(both, axis=1).astype(BF))
        out = backward(spectra, t2_ref[...], t1i_ref[...], cos_ref[...], sin_ref[...])
        for d in range(CTX):
            rows = [out[d * SUB : (d + 1) * SUB, q * FACTOR : (q + 1) * FACTOR] for q in range(4)]
            rows = jnp.concatenate(rows, axis=0).astype(BF)
            for k in range(2):
                out_ref[d, j, 48 * k : 48 * k + 32] = rows[:, k * HALF : (k + 1) * HALF]

    for d in range(CTX):
        a, b, c, e = (ref[d].astype(F32) for ref in parts)
        rows = ((a + c) + (b + e)).astype(BF)
        for j in range(Y):
            for k in range(2):
                out_ref[d, j, 48 * k + 32 : 48 * (k + 1)] = rows[:, k * HALF : (k + 1) * HALF]
    for j in range(Y):
        body(j)


def place_kernel(r_ref, a_ref, b_ref, g_ref, put, grad, sems):
    outer, sort = ones_at(subs_first), ones_at(to_subs)

    def sorted_rows(order, first, count, at, size):
        halves = [
            r_ref[first : first + count, at + 48 * k : at + 48 * k + size].reshape(FACTOR, HALF) for k in range(2)
        ]
        return mm(order, jnp.concatenate(halves, axis=1))

    turned = [sorted_rows(sort, 8 * k, 8, 0, 32).astype(BF) for k in range(8)]
    grads = [sorted_rows(outer, 16 * k, 16, 32, 16) for k in range(4)]
    gives = []
    for n in range(SUB):
        chunk = pl.ds(n * FACTOR, FACTOR)
        for s in range(2):
            at = n * 32 + s * 16
            put[s, chunk] = jnp.concatenate([t[at : at + 16] for t in turned], axis=0).T
        grad[chunk] = jnp.concatenate([t[n * 32 : (n + 1) * 32] for t in grads], axis=0).T
        for k, (src, dst) in enumerate(((put.at[0], a_ref), (put.at[1], b_ref), (grad, g_ref))):
            give = pltpu.make_async_copy(src.at[chunk], dst.at[chunk], sems.at[3 * n + k])
            give.start()
            gives.append(give)
    for give in gives:
        give.wait()


def call(kernel, outs, scratch, flops, *args, ins=None, space=pltpu.VMEM, limit=24 * 1024 * 1024):
    return pl.pallas_call(
        kernel,
        in_specs=[
            pl.BlockSpec(memory_space=pltpu.SMEM if a.dtype == jnp.int32 else ins or pltpu.VMEM) for a in args
        ],
        out_specs=[pl.BlockSpec(memory_space=space)] * len(outs),
        out_shape=[jax.ShapeDtypeStruct(*o) for o in outs],
        scratch_shapes=scratch,
        compiler_params=pltpu.CompilerParams(vmem_limit_bytes=limit),
        cost_estimate=pl.CostEstimate(flops=flops, bytes_accessed=3 << 20, transcendentals=0),
    )(*args)


def handed(x, k):
    pairs = [(a * CTX + b, b * CTX + a // Y * Y + (a ^ 2 * k) % Y) for a in range(CTX) for b in range(CTX)]
    return lax.ppermute(x, ("ctx", "zh", "y"), pairs)


def local(seq_input, out_grad, filters):
    first, second, back_last, tw_cos, tw_sin = tables()
    my_ctx = lax.axis_index("ctx")

    taps = filters.T.reshape(2, 2, PAIR * SUB, FACTOR)
    core, row = my_ctx % 2, my_ctx // 2 % 2
    mine = lax.dynamic_index_in_dim(taps, core, 1, keepdims=False)
    other = lax.dynamic_index_in_dim(taps, 1 - core, 1, keepdims=False)
    other = lax.ppermute(other, "ctx", [(a, a ^ 1) for a in range(CTX)])
    taps = jnp.stack([mine, other], axis=1)
    taps = [handed(lax.dynamic_index_in_dim(taps, row ^ k, 0, keepdims=False), k) for k in range(2)]
    (spread,) = call(
        spread_kernel,
        [((CTX * Y, 64, HALF), BF)],
        [
            pltpu.VMEM((2, TOK, HALF), BF),
            pltpu.VMEM((CTX * Y, 64, HALF), BF),
            pltpu.SemaphoreType.DMA((2 * SUB,)),
            pltpu.SemaphoreType.DMA((SUB,)),
        ],
        4 * 256 * 256 * 2048,
        seq_input,
        out_grad,
        ins=pl.ANY,
        space=pl.ANY,
        limit=LARGE,
    )
    arrived = lax.all_to_all(spread, ("ctx", "y"), 0, 0, tiled=True)
    spec, partial = call(
        forward_kernel,
        [((Y, 4 * HALF, 2 * FACTOR), BF), ((CTX, CTX, FACTOR), BF)],
        [pltpu.VMEM((PAIR, HALF, 2 * FACTOR), F32)],
        2 * 18 * 42 * 10**6,
        arrived,
        first,
        second,
        back_last,
        tw_cos,
        tw_sin,
    )
    (partial,) = call(
        pack_kernel,
        [((CTX + Y, CTX, FACTOR), BF)],
        [],
        1 << 10,
        partial,
        *taps,
        limit=4 << 20,
    )
    partial = lax.all_gather(partial, "zh", axis=0)
    (leaving,) = call(
        backward_kernel,
        [((CTX, Y, 96, HALF), BF)],
        [pltpu.VMEM((PAIR * HALF, 2 * FACTOR), F32)],
        2 * 18 * 42 * 10**6,
        spec,
        partial,
        lax.axis_index("y").reshape(1),
        first,
        second,
        back_last,
        tw_cos,
        tw_sin,
    )
    back = lax.all_to_all(leaving.reshape(CTX * Y, 96, HALF), ("ctx", "y"), 0, 0, tiled=True)
    return call(
        place_kernel,
        [((TOK, HALF), BF), ((TOK, HALF), BF), ((TOK, HALF), F32)],
        [
            pltpu.VMEM((2, TOK, HALF), BF),
            pltpu.VMEM((TOK, HALF), F32),
            pltpu.SemaphoreType.DMA((3 * SUB,)),
        ],
        6 * 256 * 256 * 2048,
        back,
        space=pl.ANY,
    )


def solution(mesh):
    inner = Mesh(mesh.devices.reshape(CTX, ZH, Y), ("ctx", "zh", "y"))
    placed = P("ctx", ("zh", "y"))
    return jax.shard_map(
        local,
        mesh=inner,
        in_specs=(placed, placed, placed),
        out_specs=(placed, placed, P("ctx", None)),
        check_vma=False,
    )
```

```python
import math

import jax
import jax.numpy as jnp
import numpy as np
from jax import lax
from jax.experimental import pallas as pl
from jax.experimental.pallas import tpu as pltpu
from jax.sharding import Mesh
from jax.sharding import PartitionSpec as P

BF = jnp.bfloat16
F32 = jnp.float32
FACTOR = 256
HALF = 128
FULL = FACTOR * FACTOR
CTX = 16
SUB = HALF // CTX
TOK = SUB * FACTOR
PAIR = 2
ZH = 4
Y = 4
LARGE = 60 * 1024 * 1024
GRAD_SCALE = 1.0 / math.sqrt(524288)


def unit(product, modulus):
    angles = np.float32(2.0 * math.pi / modulus) * (product % modulus).astype(np.float32)
    return np.cos(angles).astype(np.float32), np.sin(angles).astype(np.float32)


def tables():
    n1 = np.arange(HALF)
    k1 = np.arange(HALF)
    n2 = np.arange(FACTOR)
    cos1, sin1 = unit((2 * k1[:, None] + 1) * n1[None, :], 2 * FACTOR)
    cos2, sin2 = unit(n2[:, None] * n2[None, :], FACTOR)
    tw_cos, tw_sin = unit((2 * k1[:, None] + 1) * n2[None, :], 2 * FULL)
    first = np.concatenate([cos1, -sin1], 0)
    second = np.block([[cos2, -sin2], [sin2, cos2]])
    back_last = np.concatenate([cos1.T, -sin1.T], 1) * np.float32(2.0 / FULL)
    half = lambda a: jnp.asarray(a, dtype=BF)
    return half(first), half(second), half(back_last), jnp.asarray(tw_cos), jnp.asarray(tw_sin)


def mm(a, b):
    return jnp.dot(a, b, preferred_element_type=F32)


def ones_at(row_of, size=FACTOR):
    row = lax.broadcasted_iota(jnp.int32, (size, size), 0)
    col = lax.broadcasted_iota(jnp.int32, (size, size), 1)
    return (col == row_of(row)).astype(F32).astype(BF)


def to_owners(r):
    return (r & 7) * 32 + ((r >> 4) & 1) * 16 + (r >> 5) * PAIR + ((r >> 3) & 1)


def to_subs(r):
    return ((r >> 1) & 7) * 32 + ((r >> 4) & 1) * 16 + (r & 1) * 8 + (r >> 5)


def subs_first(r):
    return (r & 31) * SUB + (r >> 5)


def twist(first, cos, sin):
    real, imag = first[:HALF], first[HALF:]
    return jnp.concatenate([real * cos + imag * sin, imag * cos - real * sin], axis=1).astype(BF)


def untwist(first, cos, sin):
    real, imag = first[:, :FACTOR], first[:, FACTOR:]
    return jnp.concatenate([real * cos + imag * sin, real * sin - imag * cos], axis=0).astype(BF)


def split(spec):
    return spec[:, :FACTOR].astype(F32), spec[:, FACTOR:].astype(F32)


def forward(columns, t1, t2, cos, sin):
    first = mm(t1, jnp.concatenate(columns, axis=1))
    count = len(columns)
    second = [twist(first[:, k * FACTOR : (k + 1) * FACTOR], cos, sin) for k in range(count)]
    return mm(jnp.concatenate(second, axis=0), t2)


def backward(spectra, t2, t1i, cos, sin):
    first = mm(jnp.concatenate(spectra, axis=0), t2)
    count = len(spectra)
    back = [untwist(first[k * HALF : (k + 1) * HALF], cos, sin) for k in range(count)]
    return mm(t1i, jnp.concatenate(back, axis=1))


def spread_kernel(x_ref, dy_ref, out_ref, held, put, in_sems, out_sems):
    takes = []
    for n in range(SUB // 2):
        chunk = pl.ds(2 * n * FACTOR, 2 * FACTOR)
        for s, ref in enumerate((x_ref, dy_ref)):
            take = pltpu.make_async_copy(ref.at[chunk], held.at[s, chunk], in_sems.at[2 * n + s])
            take.start()
            takes.append(take)
    sort = ones_at(to_owners)
    turned = []
    for n in range(SUB):
        if n % 2 == 0:
            takes[n].wait()
            takes[n + 1].wait()
        turned.append([held[s, n * FACTOR : (n + 1) * FACTOR].T for s in range(2)])
    gives = []
    for g in range(SUB):
        chunk = pl.ds(g * SUB, SUB)
        rows = jnp.concatenate([t[g * 16 : (g + 1) * 16] for pair in turned for t in pair], axis=0)
        rows = mm(sort, rows).astype(BF)
        for k in range(2):
            put[chunk, 32 * k : 32 * (k + 1)] = rows[:, k * HALF : (k + 1) * HALF].reshape(SUB, 32, HALF)
        if g % 2 == 1:
            chunk = pl.ds((g - 1) * SUB, 2 * SUB)
            give = pltpu.make_async_copy(put.at[chunk], out_ref.at[chunk], out_sems.at[g])
            give.start()
            gives.append(give)
    for give in gives:
        give.wait()


def forward_kernel(r_ref, t1_ref, t2_ref, t1i_ref, cos_ref, sin_ref, spec_ref, g_ref, acc_ref):
    acc_ref[...] = jnp.zeros_like(acc_ref)

    for both in range(0, Y, 2):
        columns = []
        for j in (both, both + 1):
            tiles = [
                jnp.concatenate([r_ref[i * Y + j, :32], r_ref[i * Y + j, 32:]], axis=1).astype(F32)
                for i in range(CTX)
            ]
            for q in range(4):
                rows = [t[q * SUB : (q + 1) * SUB] for t in tiles]
                columns.append(jnp.concatenate(rows, axis=0).astype(BF))
        spectra = forward(columns, t1_ref[...], t2_ref[...], cos_ref[...], sin_ref[...])
        for j in (both, both + 1):
            spec = spectra[(j - both) * 4 * HALF : (j - both + 1) * 4 * HALF]
            spec_ref[j] = spec.astype(BF)
            for f in range(PAIR):
                x_real, x_imag = split(spec[f * HALF : (f + 1) * HALF])
                dy_real, dy_imag = split(spec[(PAIR + f) * HALF : (PAIR + f + 1) * HALF])
                acc_ref[f] += jnp.concatenate(
                    [dy_real * x_real + dy_imag * x_imag, dy_real * x_imag - dy_imag * x_real], axis=1
                )
    groups = [acc_ref[f].astype(BF) for f in range(PAIR)]
    out = backward(groups, t2_ref[...], t1i_ref[...], cos_ref[...], sin_ref[...]) * GRAD_SCALE
    for d in range(CTX):
        rows = [out[d * SUB : (d + 1) * SUB, f * FACTOR : (f + 1) * FACTOR] for f in range(PAIR)]
        g_ref[d] = jnp.concatenate(rows, axis=0).astype(BF)


def pack_kernel(part_ref, a_ref, b_ref, out_ref):
    out_ref[:CTX] = part_ref[...]
    out_ref[CTX : CTX + 2] = a_ref[...]
    out_ref[CTX + 2 :] = b_ref[...]


def backward_kernel(
    spec_ref, all_ref, me_ref, t1_ref, t2_ref, t1i_ref, cos_ref, sin_ref, out_ref, h_ref
):
    my_y = me_ref[0]
    parts = [all_ref.at[z] for z in range(ZH)]

    def arrival(r):
        block = r >> 3
        return ((block >> 2 << 2) + ((block & 3) ^ my_y)) * SUB + (r & 7)

    order = ones_at(arrival, HALF)
    tiles = [ref[CTX + k].astype(F32) for ref in parts for k in range(Y)]
    taps = [jnp.concatenate([t[f * SUB : (f + 1) * SUB] for t in tiles], axis=0).astype(BF) for f in range(PAIR)]
    taps = mm(order, jnp.concatenate(taps, axis=1)).astype(BF)
    columns = [taps[:, f * FACTOR : (f + 1) * FACTOR] for f in range(PAIR)]
    h_ref[...] = forward(columns, t1_ref[...], t2_ref[...], cos_ref[...], sin_ref[...])

    for both in range(0, Y, 2):
        spectra = []
        for j in (both, both + 1):
            for s in range(2):
                for f in range(PAIR):
                    at = (s * PAIR + f) * HALF
                    real, imag = split(spec_ref[j, at : at + HALF])
                    h_real, h_imag = split(h_ref[f * HALF : (f + 1) * HALF])
                    if s == 0:
                        pair = [real * h_real - imag * h_imag, -(real * h_imag + imag * h_real)]
                    else:
                        pair = [real * h_real + imag * h_imag, real * h_imag - imag * h_real]
                    spectra.append(jnp.concatenate(pair, axis=1).astype(BF))
        out = backward(spectra, t2_ref[...], t1i_ref[...], cos_ref[...], sin_ref[...])
        for j in (both, both + 1):
            for d in range(CTX):
                first = (j - both) * 4
                rows = [
                    out[d * SUB : (d + 1) * SUB, q * FACTOR : (q + 1) * FACTOR] for q in range(first, first + 4)
                ]
                rows = jnp.concatenate(rows, axis=0).astype(BF)
                for k in range(2):
                    out_ref[d, j, 48 * k : 48 * k + 32] = rows[:, k * HALF : (k + 1) * HALF]

    for d in range(CTX):
        a, b, c, e = (ref[d].astype(F32) for ref in parts)
        rows = ((a + c) + (b + e)).astype(BF)
        for j in range(Y):
            for k in range(2):
                out_ref[d, j, 48 * k + 32 : 48 * (k + 1)] = rows[:, k * HALF : (k + 1) * HALF]


def place_kernel(r_ref, a_ref, b_ref, g_ref, put, grad, sems):
    outer, sort = ones_at(subs_first), ones_at(to_subs)

    def sorted_rows(order, first, count, at, size):
        halves = [
            r_ref[first : first + count, at + 48 * k : at + 48 * k + size].reshape(FACTOR, HALF) for k in range(2)
        ]
        return mm(order, jnp.concatenate(halves, axis=1))

    gives = []

    def send(src, dst, n, k):
        chunk = pl.ds(n * FACTOR, FACTOR)
        give = pltpu.make_async_copy(src.at[chunk], dst.at[chunk], sems.at[3 * n + k])
        give.start()
        gives.append(give)

    grads = [sorted_rows(outer, 16 * k, 16, 32, 16).astype(BF) for k in range(4)]
    for n in range(SUB):
        rows = jnp.concatenate([t[n * 32 : (n + 1) * 32] for t in grads], axis=0)
        grad[n * FACTOR : (n + 1) * FACTOR] = rows.T.astype(F32)
        send(grad, g_ref, n, 2)
    turned = [sorted_rows(sort, 8 * k, 8, 0, 32).astype(BF) for k in range(8)]
    for n in range(SUB):
        for s, dst in enumerate((a_ref, b_ref)):
            at = n * 32 + s * 16
            put[s, n * FACTOR : (n + 1) * FACTOR] = jnp.concatenate([t[at : at + 16] for t in turned], axis=0).T
            send(put.at[s], dst, n, s)
    for give in gives:
        give.wait()


def call(kernel, outs, scratch, flops, *args, ins=None, space=pltpu.VMEM, limit=24 * 1024 * 1024):
    return pl.pallas_call(
        kernel,
        in_specs=[
            pl.BlockSpec(memory_space=pltpu.SMEM if a.dtype == jnp.int32 else ins or pltpu.VMEM) for a in args
        ],
        out_specs=[pl.BlockSpec(memory_space=space)] * len(outs),
        out_shape=[jax.ShapeDtypeStruct(*o) for o in outs],
        scratch_shapes=scratch,
        compiler_params=pltpu.CompilerParams(vmem_limit_bytes=limit),
        cost_estimate=pl.CostEstimate(flops=flops, bytes_accessed=3 << 20, transcendentals=0),
    )(*args)


def handed(x, k):
    pairs = [(a * CTX + b, b * CTX + a // Y * Y + (a ^ 2 * k) % Y) for a in range(CTX) for b in range(CTX)]
    return lax.ppermute(x, ("ctx", "zh", "y"), pairs)


def local(seq_input, out_grad, filters):
    first, second, back_last, tw_cos, tw_sin = tables()
    my_ctx = lax.axis_index("ctx")

    taps = filters.T.reshape(2, 2, PAIR * SUB, FACTOR)
    core, row = my_ctx % 2, my_ctx // 2 % 2
    mine = lax.dynamic_index_in_dim(taps, core, 1, keepdims=False)
    other = lax.dynamic_index_in_dim(taps, 1 - core, 1, keepdims=False)
    other = lax.ppermute(other, "ctx", [(a, a ^ 1) for a in range(CTX)])
    taps = jnp.stack([mine, other], axis=1)
    taps = [handed(lax.dynamic_index_in_dim(taps, row ^ k, 0, keepdims=False), k) for k in range(2)]
    (spread,) = call(
        spread_kernel,
        [((CTX * Y, 64, HALF), BF)],
        [
            pltpu.VMEM((2, TOK, HALF), BF),
            pltpu.VMEM((CTX * Y, 64, HALF), BF),
            pltpu.SemaphoreType.DMA((2 * SUB,)),
            pltpu.SemaphoreType.DMA((SUB,)),
        ],
        4 * 256 * 256 * 2048,
        seq_input,
        out_grad,
        ins=pl.ANY,
        space=pl.ANY,
        limit=LARGE,
    )
    arrived = lax.all_to_all(spread, ("ctx", "y"), 0, 0, tiled=True)
    spec, partial = call(
        forward_kernel,
        [((Y, 4 * HALF, 2 * FACTOR), BF), ((CTX, CTX, FACTOR), BF)],
        [pltpu.VMEM((PAIR, HALF, 2 * FACTOR), F32)],
        2 * 18 * 42 * 10**6,
        arrived,
        first,
        second,
        back_last,
        tw_cos,
        tw_sin,
    )
    (partial,) = call(
        pack_kernel,
        [((CTX + Y, CTX, FACTOR), BF)],
        [],
        1 << 10,
        partial,
        *taps,
        limit=4 << 20,
    )
    partial = lax.all_gather(partial, "zh", axis=0)
    (leaving,) = call(
        backward_kernel,
        [((CTX, Y, 96, HALF), BF)],
        [pltpu.VMEM((PAIR * HALF, 2 * FACTOR), F32)],
        2 * 18 * 42 * 10**6,
        spec,
        partial,
        lax.axis_index("y").reshape(1),
        first,
        second,
        back_last,
        tw_cos,
        tw_sin,
    )
    back = lax.all_to_all(leaving.reshape(CTX * Y, 96, HALF), ("ctx", "y"), 0, 0, tiled=True)
    return call(
        place_kernel,
        [((TOK, HALF), BF), ((TOK, HALF), BF), ((TOK, HALF), F32)],
        [
            pltpu.VMEM((2, TOK, HALF), BF),
            pltpu.VMEM((TOK, HALF), F32),
            pltpu.SemaphoreType.DMA((3 * SUB,)),
        ],
        6 * 256 * 256 * 2048,
        back,
        space=pl.ANY,
    )


def solution(mesh):
    inner = Mesh(mesh.devices.reshape(CTX, ZH, Y), ("ctx", "zh", "y"))
    placed = P("ctx", ("zh", "y"))
    return jax.shard_map(
        local,
        mesh=inner,
        in_specs=(placed, placed, placed),
        out_specs=(placed, placed, P("ctx", None)),
        check_vma=False,
    )
```

```python
import math

import jax
import jax.numpy as jnp
import numpy as np
from jax import lax
from jax.experimental import pallas as pl
from jax.experimental.pallas import tpu as pltpu
from jax.sharding import Mesh
from jax.sharding import PartitionSpec as P

BF = jnp.bfloat16
F32 = jnp.float32
FACTOR = 256
HALF = 128
FULL = FACTOR * FACTOR
CTX = 16
SUB = HALF // CTX
TOK = SUB * FACTOR
PAIR = 2
ZH = 4
Y = 4
LARGE = 60 * 1024 * 1024
GRAD_SCALE = 1.0 / math.sqrt(524288)


def unit(product, modulus):
    angles = np.float32(2.0 * math.pi / modulus) * (product % modulus).astype(np.float32)
    return np.cos(angles).astype(np.float32), np.sin(angles).astype(np.float32)


def tables():
    n1 = np.arange(HALF)
    k1 = np.arange(HALF)
    n2 = np.arange(FACTOR)
    cos1, sin1 = unit((2 * k1[:, None] + 1) * n1[None, :], 2 * FACTOR)
    cos2, sin2 = unit(n2[:, None] * n2[None, :], FACTOR)
    tw_cos, tw_sin = unit((2 * k1[:, None] + 1) * n2[None, :], 2 * FULL)
    first = np.concatenate([cos1, -sin1], 0)
    second = np.block([[cos2, -sin2], [sin2, cos2]])
    back_last = np.concatenate([cos1.T, -sin1.T], 1) * np.float32(2.0 / FULL)
    half = lambda a: jnp.asarray(a, dtype=BF)
    return half(first), half(second), half(back_last), jnp.asarray(tw_cos), jnp.asarray(tw_sin)


def mm(a, b):
    return jnp.dot(a, b, preferred_element_type=F32)


def ones_at(row_of, size=FACTOR):
    row = lax.broadcasted_iota(jnp.int32, (size, size), 0)
    col = lax.broadcasted_iota(jnp.int32, (size, size), 1)
    return (col == row_of(row)).astype(F32).astype(BF)


def to_owners(r):
    return (r & 7) * 16 + (r >> 4) * PAIR + ((r >> 3) & 1)


def to_subs(r):
    return ((r >> 1) & 7) * 32 + ((r >> 4) & 1) * 16 + (r & 1) * 8 + (r >> 5)


def subs_first(r):
    return (r & 31) * SUB + (r >> 5)


def twist(first, cos, sin):
    real, imag = first[:HALF], first[HALF:]
    return jnp.concatenate([real * cos + imag * sin, imag * cos - real * sin], axis=1).astype(BF)


def untwist(first, cos, sin):
    real, imag = first[:, :FACTOR], first[:, FACTOR:]
    return jnp.concatenate([real * cos + imag * sin, real * sin - imag * cos], axis=0).astype(BF)


def split(spec):
    return spec[:, :FACTOR].astype(F32), spec[:, FACTOR:].astype(F32)


def forward(columns, t1, t2, cos, sin):
    first = mm(t1, jnp.concatenate(columns, axis=1))
    count = len(columns)
    second = [twist(first[:, k * FACTOR : (k + 1) * FACTOR], cos, sin) for k in range(count)]
    return mm(jnp.concatenate(second, axis=0), t2)


def backward(spectra, t2, t1i, cos, sin):
    first = mm(jnp.concatenate(spectra, axis=0), t2)
    count = len(spectra)
    back = [untwist(first[k * HALF : (k + 1) * HALF], cos, sin) for k in range(count)]
    return mm(t1i, jnp.concatenate(back, axis=1))


def spread_kernel(x_ref, dy_ref, out_ref, held, put, in_sems, out_sems):
    half = SUB // 2
    takes = []
    for s, ref in enumerate((x_ref, dy_ref)):
        for n in range(half):
            chunk = pl.ds(2 * n * FACTOR, 2 * FACTOR)
            take = pltpu.make_async_copy(ref.at[chunk], held.at[s, chunk], in_sems.at[half * s + n])
            take.start()
            takes.append(take)
    sort = ones_at(to_owners, HALF)
    gives = []
    for s in range(2):
        turned = []
        for n in range(SUB):
            if n % 2 == 0:
                takes[half * s + n // 2].wait()
            turned.append(held[s, n * FACTOR : (n + 1) * FACTOR].T)
        for g in range(SUB):
            rows = jnp.concatenate([t[g * 16 : (g + 1) * 16] for t in turned], axis=0)
            rows = mm(sort, rows).astype(BF)
            for k in range(2):
                part = rows[:, k * HALF : (k + 1) * HALF].reshape(SUB, 16, HALF)
                put[s, g * SUB : (g + 1) * SUB, 16 * k : 16 * (k + 1)] = part
            if g % 4 == 3:
                chunk = pl.ds((g - 3) * SUB, 4 * SUB)
                give = pltpu.make_async_copy(
                    put.at[s, chunk], out_ref.at[chunk, pl.ds(32 * s, 32)], out_sems.at[2 * s + g // 4]
                )
                give.start()
                gives.append(give)
    for give in gives:
        give.wait()


def arrived_rows(r_ref, owner, s):
    at = 32 * s
    return jnp.concatenate([r_ref[owner, at : at + 16], r_ref[owner, at + 16 : at + 32]], axis=1)


def forward_kernel(r_ref, t1_ref, t2_ref, t1i_ref, cos_ref, sin_ref, spec_ref, g_ref, acc_ref):
    acc_ref[...] = jnp.zeros_like(acc_ref)

    for both in range(0, Y, 2):
        columns = []
        for j in (both, both + 1):
            tiles = [
                jnp.concatenate([arrived_rows(r_ref, i * Y + j, s) for s in range(2)], axis=0).astype(F32)
                for i in range(CTX)
            ]
            for q in range(4):
                rows = [t[q * SUB : (q + 1) * SUB] for t in tiles]
                columns.append(jnp.concatenate(rows, axis=0).astype(BF))
        spectra = forward(columns, t1_ref[...], t2_ref[...], cos_ref[...], sin_ref[...])
        for j in (both, both + 1):
            spec = spectra[(j - both) * 4 * HALF : (j - both + 1) * 4 * HALF]
            spec_ref[j] = spec.astype(BF)
            for f in range(PAIR):
                x_real, x_imag = split(spec[f * HALF : (f + 1) * HALF])
                dy_real, dy_imag = split(spec[(PAIR + f) * HALF : (PAIR + f + 1) * HALF])
                acc_ref[f] += jnp.concatenate(
                    [dy_real * x_real + dy_imag * x_imag, dy_real * x_imag - dy_imag * x_real], axis=1
                )
    groups = [acc_ref[f].astype(BF) for f in range(PAIR)]
    out = backward(groups, t2_ref[...], t1i_ref[...], cos_ref[...], sin_ref[...]) * GRAD_SCALE
    for d in range(CTX):
        rows = [out[d * SUB : (d + 1) * SUB, f * FACTOR : (f + 1) * FACTOR] for f in range(PAIR)]
        g_ref[d] = jnp.concatenate(rows, axis=0).astype(BF)


def pack_kernel(part_ref, a_ref, b_ref, out_ref):
    out_ref[:CTX] = part_ref[...]
    out_ref[CTX : CTX + 2] = a_ref[...]
    out_ref[CTX + 2 :] = b_ref[...]


def backward_kernel(
    spec_ref, all_ref, me_ref, t1_ref, t2_ref, t1i_ref, cos_ref, sin_ref, out_ref, h_ref
):
    my_y = me_ref[0]
    parts = [all_ref.at[z] for z in range(ZH)]

    def arrival(r):
        block = r >> 3
        return ((block >> 2 << 2) + ((block & 3) ^ my_y)) * SUB + (r & 7)

    order = ones_at(arrival, HALF)
    tiles = [ref[CTX + k].astype(F32) for ref in parts for k in range(Y)]
    taps = [jnp.concatenate([t[f * SUB : (f + 1) * SUB] for t in tiles], axis=0).astype(BF) for f in range(PAIR)]
    taps = mm(order, jnp.concatenate(taps, axis=1)).astype(BF)
    columns = [taps[:, f * FACTOR : (f + 1) * FACTOR] for f in range(PAIR)]
    h_ref[...] = forward(columns, t1_ref[...], t2_ref[...], cos_ref[...], sin_ref[...])

    for both in range(0, Y, 2):
        spectra = []
        for j in (both, both + 1):
            for s in range(2):
                for f in range(PAIR):
                    at = (s * PAIR + f) * HALF
                    real, imag = split(spec_ref[j, at : at + HALF])
                    h_real, h_imag = split(h_ref[f * HALF : (f + 1) * HALF])
                    if s == 0:
                        pair = [real * h_real - imag * h_imag, -(real * h_imag + imag * h_real)]
                    else:
                        pair = [real * h_real + imag * h_imag, real * h_imag - imag * h_real]
                    spectra.append(jnp.concatenate(pair, axis=1).astype(BF))
        out = backward(spectra, t2_ref[...], t1i_ref[...], cos_ref[...], sin_ref[...])
        for j in (both, both + 1):
            for d in range(CTX):
                first = (j - both) * 4
                rows = [
                    out[d * SUB : (d + 1) * SUB, q * FACTOR : (q + 1) * FACTOR] for q in range(first, first + 4)
                ]
                rows = jnp.concatenate(rows, axis=0).astype(BF)
                for k in range(2):
                    out_ref[d, j, 48 * k : 48 * k + 32] = rows[:, k * HALF : (k + 1) * HALF]

    for d in range(CTX):
        a, b, c, e = (ref[d].astype(F32) for ref in parts)
        rows = ((a + c) + (b + e)).astype(BF)
        for j in range(Y):
            for k in range(2):
                out_ref[d, j, 48 * k + 32 : 48 * (k + 1)] = rows[:, k * HALF : (k + 1) * HALF]


def place_kernel(r_ref, a_ref, b_ref, g_ref, put, grad, sems):
    outer, sort = ones_at(subs_first), ones_at(to_subs)

    def sorted_rows(order, first, count, at, size):
        halves = [
            r_ref[first : first + count, at + 48 * k : at + 48 * k + size].reshape(FACTOR, HALF) for k in range(2)
        ]
        return mm(order, jnp.concatenate(halves, axis=1))

    gives = []

    def send(src, dst, n, k):
        chunk = pl.ds(n * FACTOR, FACTOR)
        give = pltpu.make_async_copy(src.at[chunk], dst.at[chunk], sems.at[3 * n + k])
        give.start()
        gives.append(give)

    grads = [sorted_rows(outer, 16 * k, 16, 32, 16).astype(BF) for k in range(4)]
    for n in range(SUB):
        rows = jnp.concatenate([t[n * 32 : (n + 1) * 32] for t in grads], axis=0)
        grad[n * FACTOR : (n + 1) * FACTOR] = rows.T.astype(F32)
        send(grad, g_ref, n, 2)
    turned = [sorted_rows(sort, 8 * k, 8, 0, 32).astype(BF) for k in range(8)]
    for n in range(SUB):
        for s, dst in enumerate((a_ref, b_ref)):
            at = n * 32 + s * 16
            put[s, n * FACTOR : (n + 1) * FACTOR] = jnp.concatenate([t[at : at + 16] for t in turned], axis=0).T
            send(put.at[s], dst, n, s)
    for give in gives:
        give.wait()


def call(kernel, outs, scratch, flops, *args, ins=None, space=pltpu.VMEM, limit=24 * 1024 * 1024):
    return pl.pallas_call(
        kernel,
        in_specs=[
            pl.BlockSpec(memory_space=pltpu.SMEM if a.dtype == jnp.int32 else ins or pltpu.VMEM) for a in args
        ],
        out_specs=[pl.BlockSpec(memory_space=space)] * len(outs),
        out_shape=[jax.ShapeDtypeStruct(*o) for o in outs],
        scratch_shapes=scratch,
        compiler_params=pltpu.CompilerParams(vmem_limit_bytes=limit),
        cost_estimate=pl.CostEstimate(flops=flops, bytes_accessed=3 << 20, transcendentals=0),
    )(*args)


def handed(x, k):
    pairs = [(a * CTX + b, b * CTX + a // Y * Y + (a ^ 2 * k) % Y) for a in range(CTX) for b in range(CTX)]
    return lax.ppermute(x, ("ctx", "zh", "y"), pairs)


def local(seq_input, out_grad, filters):
    first, second, back_last, tw_cos, tw_sin = tables()
    my_ctx = lax.axis_index("ctx")

    taps = filters.T.reshape(2, 2, PAIR * SUB, FACTOR)
    core, row = my_ctx % 2, my_ctx // 2 % 2
    mine = lax.dynamic_index_in_dim(taps, core, 1, keepdims=False)
    other = lax.dynamic_index_in_dim(taps, 1 - core, 1, keepdims=False)
    other = lax.ppermute(other, "ctx", [(a, a ^ 1) for a in range(CTX)])
    taps = jnp.stack([mine, other], axis=1)
    taps = [handed(lax.dynamic_index_in_dim(taps, row ^ k, 0, keepdims=False), k) for k in range(2)]
    (spread,) = call(
        spread_kernel,
        [((CTX * Y, 64, HALF), BF)],
        [
            pltpu.VMEM((2, TOK, HALF), BF),
            pltpu.VMEM((2, CTX * Y, 32, HALF), BF),
            pltpu.SemaphoreType.DMA((2 * SUB,)),
            pltpu.SemaphoreType.DMA((SUB,)),
        ],
        4 * 256 * 256 * 2048,
        seq_input,
        out_grad,
        ins=pl.ANY,
        space=pl.ANY,
        limit=LARGE,
    )
    arrived = lax.all_to_all(spread, ("ctx", "y"), 0, 0, tiled=True)
    spec, partial = call(
        forward_kernel,
        [((Y, 4 * HALF, 2 * FACTOR), BF), ((CTX, CTX, FACTOR), BF)],
        [pltpu.VMEM((PAIR, HALF, 2 * FACTOR), F32)],
        2 * 18 * 42 * 10**6,
        arrived,
        first,
        second,
        back_last,
        tw_cos,
        tw_sin,
    )
    (partial,) = call(
        pack_kernel,
        [((CTX + Y, CTX, FACTOR), BF)],
        [],
        1 << 10,
        partial,
        *taps,
        limit=4 << 20,
    )
    partial = lax.all_gather(partial, "zh", axis=0)
    (leaving,) = call(
        backward_kernel,
        [((CTX, Y, 96, HALF), BF)],
        [pltpu.VMEM((PAIR * HALF, 2 * FACTOR), F32)],
        2 * 18 * 42 * 10**6,
        spec,
        partial,
        lax.axis_index("y").reshape(1),
        first,
        second,
        back_last,
        tw_cos,
        tw_sin,
    )
    back = lax.all_to_all(leaving.reshape(CTX * Y, 96, HALF), ("ctx", "y"), 0, 0, tiled=True)
    return call(
        place_kernel,
        [((TOK, HALF), BF), ((TOK, HALF), BF), ((TOK, HALF), F32)],
        [
            pltpu.VMEM((2, TOK, HALF), BF),
            pltpu.VMEM((TOK, HALF), F32),
            pltpu.SemaphoreType.DMA((3 * SUB,)),
        ],
        6 * 256 * 256 * 2048,
        back,
        space=pl.ANY,
    )


def solution(mesh):
    inner = Mesh(mesh.devices.reshape(CTX, ZH, Y), ("ctx", "zh", "y"))
    placed = P("ctx", ("zh", "y"))
    return jax.shard_map(
        local,
        mesh=inner,
        in_specs=(placed, placed, placed),
        out_specs=(placed, placed, P("ctx", None)),
        check_vma=False,
    )
```

```python
import math

import jax
import jax.numpy as jnp
import numpy as np
from jax import lax
from jax.experimental import pallas as pl
from jax.experimental.pallas import tpu as pltpu
from jax.sharding import Mesh
from jax.sharding import PartitionSpec as P

BF = jnp.bfloat16
F32 = jnp.float32
FACTOR = 256
HALF = 128
FULL = FACTOR * FACTOR
CTX = 16
SUB = HALF // CTX
TOK = SUB * FACTOR
PAIR = 2
ZH = 4
Y = 4
LARGE = 60 * 1024 * 1024
GRAD_SCALE = 1.0 / math.sqrt(524288)


def unit(product, modulus):
    angles = np.float32(2.0 * math.pi / modulus) * (product % modulus).astype(np.float32)
    return np.cos(angles).astype(np.float32), np.sin(angles).astype(np.float32)


def tables():
    n1 = np.arange(HALF)
    k1 = np.arange(HALF)
    n2 = np.arange(FACTOR)
    cos1, sin1 = unit((2 * k1[:, None] + 1) * n1[None, :], 2 * FACTOR)
    cos2, sin2 = unit(n2[:, None] * n2[None, :], FACTOR)
    tw_cos, tw_sin = unit((2 * k1[:, None] + 1) * n2[None, :], 2 * FULL)
    first = np.concatenate([cos1, -sin1], 0)
    second = np.block([[cos2, -sin2], [sin2, cos2]])
    back_last = np.concatenate([cos1.T, -sin1.T], 1) * np.float32(2.0 / FULL)
    half = lambda a: jnp.asarray(a, dtype=BF)
    return half(first), half(second), half(back_last), jnp.asarray(tw_cos), jnp.asarray(tw_sin)


def mm(a, b):
    return jnp.dot(a, b, preferred_element_type=F32)


def ones_at(row_of, size=FACTOR):
    row = lax.broadcasted_iota(jnp.int32, (size, size), 0)
    col = lax.broadcasted_iota(jnp.int32, (size, size), 1)
    return (col == row_of(row)).astype(F32).astype(BF)


def to_owners(r):
    return (r & 7) * 32 + ((r >> 4) & 1) * 16 + (r >> 5) * PAIR + ((r >> 3) & 1)


def to_subs(r):
    return ((r >> 1) & 7) * 32 + ((r >> 4) & 1) * 16 + (r & 1) * 8 + (r >> 5)


def subs_first(r):
    return (r & 31) * SUB + (r >> 5)


def twist(first, cos, sin):
    real, imag = first[:HALF], first[HALF:]
    return jnp.concatenate([real * cos + imag * sin, imag * cos - real * sin], axis=1).astype(BF)


def untwist(first, cos, sin):
    real, imag = first[:, :FACTOR], first[:, FACTOR:]
    return jnp.concatenate([real * cos + imag * sin, real * sin - imag * cos], axis=0).astype(BF)


def split(spec):
    return spec[:, :FACTOR].astype(F32), spec[:, FACTOR:].astype(F32)


def forward(columns, t1, t2, cos, sin):
    first = mm(t1, jnp.concatenate(columns, axis=1))
    count = len(columns)
    second = [twist(first[:, k * FACTOR : (k + 1) * FACTOR], cos, sin) for k in range(count)]
    return mm(jnp.concatenate(second, axis=0), t2)


def backward(spectra, t2, t1i, cos, sin):
    first = mm(jnp.concatenate(spectra, axis=0), t2)
    count = len(spectra)
    back = [untwist(first[k * HALF : (k + 1) * HALF], cos, sin) for k in range(count)]
    return mm(t1i, jnp.concatenate(back, axis=1))


def spread_kernel(x_ref, dy_ref, out_ref, held, put, in_sems, out_sems):
    takes = []
    for n in range(SUB // 2):
        chunk = pl.ds(2 * n * FACTOR, 2 * FACTOR)
        for s, ref in enumerate((x_ref, dy_ref)):
            take = pltpu.make_async_copy(ref.at[chunk], held.at[s, chunk], in_sems.at[2 * n + s])
            take.start()
            takes.append(take)
    sort = ones_at(to_owners)
    turned = []
    for n in range(SUB):
        if n % 2 == 0:
            takes[n].wait()
            takes[n + 1].wait()
        turned.append([held[s, n * FACTOR : (n + 1) * FACTOR].T for s in range(2)])
    gives = []
    for g in range(SUB):
        chunk = pl.ds(g * SUB, SUB)
        rows = jnp.concatenate([t[g * 16 : (g + 1) * 16] for pair in turned for t in pair], axis=0)
        rows = mm(sort, rows).astype(BF)
        for k in range(2):
            put[chunk, 32 * k : 32 * (k + 1)] = rows[:, k * HALF : (k + 1) * HALF].reshape(SUB, 32, HALF)
        if g % 2 == 1:
            chunk = pl.ds((g - 1) * SUB, 2 * SUB)
            give = pltpu.make_async_copy(put.at[chunk], out_ref.at[chunk], out_sems.at[g])
            give.start()
            gives.append(give)
    for give in gives:
        give.wait()


def forward_kernel(r_ref, t1_ref, t2_ref, t1i_ref, cos_ref, sin_ref, spec_ref, g_ref, acc_ref):

    for both in range(0, Y, 2):
        columns = []
        for j in (both, both + 1):
            tiles = [
                jnp.concatenate([r_ref[i * Y + j, :32], r_ref[i * Y + j, 32:]], axis=1).astype(F32)
                for i in range(CTX)
            ]
            for q in range(4):
                rows = [t[q * SUB : (q + 1) * SUB] for t in tiles]
                columns.append(jnp.concatenate(rows, axis=0).astype(BF))
        spectra = forward(columns, t1_ref[...], t2_ref[...], cos_ref[...], sin_ref[...])
        for j in (both, both + 1):
            spec = spectra[(j - both) * 4 * HALF : (j - both + 1) * 4 * HALF]
            spec_ref[j] = spec.astype(BF)
            for f in range(PAIR):
                x_real, x_imag = split(spec[f * HALF : (f + 1) * HALF])
                dy_real, dy_imag = split(spec[(PAIR + f) * HALF : (PAIR + f + 1) * HALF])
                part = [dy_real * x_real + dy_imag * x_imag, dy_real * x_imag - dy_imag * x_real]
                part = jnp.concatenate(part, axis=1)
                acc_ref[f] = part if j == 0 else acc_ref[f] + part
    groups = [acc_ref[f].astype(BF) for f in range(PAIR)]
    out = backward(groups, t2_ref[...], t1i_ref[...], cos_ref[...], sin_ref[...]) * GRAD_SCALE
    for d in range(CTX):
        rows = [out[d * SUB : (d + 1) * SUB, f * FACTOR : (f + 1) * FACTOR] for f in range(PAIR)]
        g_ref[d] = jnp.concatenate(rows, axis=0).astype(BF)


def pack_kernel(part_ref, a_ref, b_ref, out_ref):
    out_ref[:CTX] = part_ref[...]
    out_ref[CTX : CTX + 2] = a_ref[...]
    out_ref[CTX + 2 :] = b_ref[...]


def backward_kernel(
    spec_ref, all_ref, me_ref, t1_ref, t2_ref, t1i_ref, cos_ref, sin_ref, out_ref, h_ref
):
    my_y = me_ref[0]
    parts = [all_ref.at[z] for z in range(ZH)]

    def arrival(r):
        block = r >> 3
        return ((block >> 2 << 2) + ((block & 3) ^ my_y)) * SUB + (r & 7)

    order = ones_at(arrival, HALF)
    tiles = [ref[CTX + k].astype(F32) for ref in parts for k in range(Y)]
    taps = [jnp.concatenate([t[f * SUB : (f + 1) * SUB] for t in tiles], axis=0).astype(BF) for f in range(PAIR)]
    taps = mm(order, jnp.concatenate(taps, axis=1)).astype(BF)
    columns = [taps[:, f * FACTOR : (f + 1) * FACTOR] for f in range(PAIR)]
    h_ref[...] = forward(columns, t1_ref[...], t2_ref[...], cos_ref[...], sin_ref[...])

    for both in range(0, Y, 2):
        spectra = []
        for j in (both, both + 1):
            for s in range(2):
                for f in range(PAIR):
                    at = (s * PAIR + f) * HALF
                    real, imag = split(spec_ref[j, at : at + HALF])
                    h_real, h_imag = split(h_ref[f * HALF : (f + 1) * HALF])
                    if s == 0:
                        pair = [real * h_real - imag * h_imag, -(real * h_imag + imag * h_real)]
                    else:
                        pair = [real * h_real + imag * h_imag, real * h_imag - imag * h_real]
                    spectra.append(jnp.concatenate(pair, axis=1).astype(BF))
        out = backward(spectra, t2_ref[...], t1i_ref[...], cos_ref[...], sin_ref[...])
        for j in (both, both + 1):
            for d in range(CTX):
                first = (j - both) * 4
                rows = [
                    out[d * SUB : (d + 1) * SUB, q * FACTOR : (q + 1) * FACTOR] for q in range(first, first + 4)
                ]
                rows = jnp.concatenate(rows, axis=0).astype(BF)
                for k in range(2):
                    out_ref[d, j, 48 * k : 48 * k + 32] = rows[:, k * HALF : (k + 1) * HALF]

    for d in range(CTX):
        a, b, c, e = (ref[d].astype(F32) for ref in parts)
        rows = ((a + c) + (b + e)).astype(BF)
        for j in range(Y):
            for k in range(2):
                out_ref[d, j, 48 * k + 32 : 48 * (k + 1)] = rows[:, k * HALF : (k + 1) * HALF]


def place_kernel(r_ref, a_ref, b_ref, g_ref, put, grad, sems):
    outer, sort = ones_at(subs_first), ones_at(to_subs)

    def sorted_rows(order, first, count, at, size):
        halves = [
            r_ref[first : first + count, at + 48 * k : at + 48 * k + size].reshape(FACTOR, HALF) for k in range(2)
        ]
        return mm(order, jnp.concatenate(halves, axis=1))

    gives = []

    def send(src, dst, n, k):
        chunk = pl.ds(n * FACTOR, FACTOR)
        give = pltpu.make_async_copy(src.at[chunk], dst.at[chunk], sems.at[3 * n + k])
        give.start()
        gives.append(give)

    grads = [sorted_rows(outer, 16 * k, 16, 32, 16).astype(BF) for k in range(4)]
    for n in range(SUB):
        rows = jnp.concatenate([t[n * 32 : (n + 1) * 32] for t in grads], axis=0)
        grad[n * FACTOR : (n + 1) * FACTOR] = rows.T.astype(F32)
        send(grad, g_ref, n, 2)
    turned = [sorted_rows(sort, 8 * k, 8, 0, 32).astype(BF) for k in range(8)]
    for n in range(SUB):
        for s, dst in enumerate((a_ref, b_ref)):
            at = n * 32 + s * 16
            put[s, n * FACTOR : (n + 1) * FACTOR] = jnp.concatenate([t[at : at + 16] for t in turned], axis=0).T
            send(put.at[s], dst, n, s)
    for give in gives:
        give.wait()


def call(kernel, outs, scratch, flops, *args, ins=None, space=pltpu.VMEM, limit=24 * 1024 * 1024):
    return pl.pallas_call(
        kernel,
        in_specs=[
            pl.BlockSpec(memory_space=pltpu.SMEM if a.dtype == jnp.int32 else ins or pltpu.VMEM) for a in args
        ],
        out_specs=[pl.BlockSpec(memory_space=space)] * len(outs),
        out_shape=[jax.ShapeDtypeStruct(*o) for o in outs],
        scratch_shapes=scratch,
        compiler_params=pltpu.CompilerParams(vmem_limit_bytes=limit),
        cost_estimate=pl.CostEstimate(flops=flops, bytes_accessed=3 << 20, transcendentals=0),
    )(*args)


def handed(x, k):
    pairs = [(a * CTX + b, b * CTX + a // Y * Y + (a ^ 2 * k) % Y) for a in range(CTX) for b in range(CTX)]
    return lax.ppermute(x, ("ctx", "zh", "y"), pairs)


def local(seq_input, out_grad, filters):
    first, second, back_last, tw_cos, tw_sin = tables()
    my_ctx = lax.axis_index("ctx")

    taps = filters.T.reshape(2, 2, PAIR * SUB, FACTOR)
    core, row = my_ctx % 2, my_ctx // 2 % 2
    mine = lax.dynamic_index_in_dim(taps, core, 1, keepdims=False)
    other = lax.dynamic_index_in_dim(taps, 1 - core, 1, keepdims=False)
    other = lax.ppermute(other, "ctx", [(a, a ^ 1) for a in range(CTX)])
    taps = jnp.stack([mine, other], axis=1)
    taps = [handed(lax.dynamic_index_in_dim(taps, row ^ k, 0, keepdims=False), k) for k in range(2)]
    (spread,) = call(
        spread_kernel,
        [((CTX * Y, 64, HALF), BF)],
        [
            pltpu.VMEM((2, TOK, HALF), BF),
            pltpu.VMEM((CTX * Y, 64, HALF), BF),
            pltpu.SemaphoreType.DMA((2 * SUB,)),
            pltpu.SemaphoreType.DMA((SUB,)),
        ],
        4 * 256 * 256 * 2048,
        seq_input,
        out_grad,
        ins=pl.ANY,
        space=pl.ANY,
        limit=LARGE,
    )
    arrived = lax.all_to_all(spread, ("ctx", "y"), 0, 0, tiled=True)
    spec, partial = call(
        forward_kernel,
        [((Y, 4 * HALF, 2 * FACTOR), BF), ((CTX, CTX, FACTOR), BF)],
        [pltpu.VMEM((PAIR, HALF, 2 * FACTOR), F32)],
        2 * 18 * 42 * 10**6,
        arrived,
        first,
        second,
        back_last,
        tw_cos,
        tw_sin,
    )
    (partial,) = call(
        pack_kernel,
        [((CTX + Y, CTX, FACTOR), BF)],
        [],
        1 << 10,
        partial,
        *taps,
        limit=4 << 20,
    )
    partial = lax.all_gather(partial, "zh", axis=0)
    (leaving,) = call(
        backward_kernel,
        [((CTX, Y, 96, HALF), BF)],
        [pltpu.VMEM((PAIR * HALF, 2 * FACTOR), F32)],
        2 * 18 * 42 * 10**6,
        spec,
        partial,
        lax.axis_index("y").reshape(1),
        first,
        second,
        back_last,
        tw_cos,
        tw_sin,
    )
    back = lax.all_to_all(leaving.reshape(CTX * Y, 96, HALF), ("ctx", "y"), 0, 0, tiled=True)
    return call(
        place_kernel,
        [((TOK, HALF), BF), ((TOK, HALF), BF), ((TOK, HALF), F32)],
        [
            pltpu.VMEM((2, TOK, HALF), BF),
            pltpu.VMEM((TOK, HALF), F32),
            pltpu.SemaphoreType.DMA((3 * SUB,)),
        ],
        6 * 256 * 256 * 2048,
        back,
        space=pl.ANY,
    )


def solution(mesh):
    inner = Mesh(mesh.devices.reshape(CTX, ZH, Y), ("ctx", "zh", "y"))
    placed = P("ctx", ("zh", "y"))
    return jax.shard_map(
        local,
        mesh=inner,
        in_specs=(placed, placed, placed),
        out_specs=(placed, placed, P("ctx", None)),
        check_vma=False,
    )
```
